32 devices in a mesh: groups: 2 (over y), seq: 16 (over z, x, core), mp: 1.
Axes of the slice: x: 2, y: 2, z: 4, core: 2. Of those that a mesh axis runs over, the one named last changes fastest.
Arguments:
- student: bfloat16 [32768, 2048], P(('groups', 'seq'), 'mp'), parts along dimension 0, may hold values from -68 to 68
- teacher: bfloat16 [8192, 4096], P(('groups', 'seq'), 'mp'), parts along dimension 0, may hold values from -6 to 6
- weight: bfloat16 [4096, 2048], P('seq', 'mp'), may hold values from -0.09375 to 0.09375
- cotangent: bfloat16 [32768, 2048], P(('groups', 'seq'), 'mp'), parts along dimension 0, may hold values from -6 to 6
- block_map: int32 [256, 2], P('groups'), parts along dimension 0, may hold values from 0 to 31, as said below
- span_begin: int32 [32768], P(('groups', 'seq')), parts along dimension 0, may hold values from 0 to 255, as said below
- span_stop: int32 [32768], P(('groups', 'seq')), parts along dimension 0, may hold values from 1 to 256
Outputs:
- attended: bfloat16 [32768, 2048], P(('groups', 'seq'), 'mp'), parts along dimension 0
- student_grad: bfloat16 [32768, 2048], P(('groups', 'seq'), 'mp'), parts along dimension 0
- weight_grad: float32 [8192, 2048], P(('groups', 'seq'), 'mp'), parts along dimension 0
The draws below stay inside these ranges and needn't reach their ends.
There are 2 independent parts, one for each index of `groups`. The reference program is written for one: setup_inputs(seed, part) draws one part's arguments, and reference() takes and returns one part's arrays. A program takes and returns all parts, laid end to end along the dimension named above; an argument that names none is the same for every part. Nothing has to cross between parts.
Inputs may be any that keep to these rules, and one draw needn't show every extreme that they name: `block_map`: teacher block m lies on teacher device m // 2. The student blocks of one device (1024 / 128 of them) name at most 1 block of one teacher device in all their entries together, and exactly 1 of some teacher device. An offset into the 256 key rows of the row's student block; span_begin < span_stop <= span_begin + 4.
All inputs are finite; a program needn't handle non-finite values.
Results may differ from the reference program's by a relative error of at most 0.007.
The reference program's roundings to bfloat16 on the way count: a program that leaves them out, or rounds other values in their place, can miss the bound.
Values may be sent and summed in bfloat16 or wider, within the bound.
A program may use at most 192 MiB of HBM per device.

```python
import jax
import jax.numpy as jnp
from jax import lax

DS = 2048
HEAD = 128
DT = 4096
BLK = 128
NB = 2
SPAN_MAX = 4
S_DEV = 1024
T_DEV = 256
ST = 16384
TT = 4096
SBLOCKS = 128
TBLOCKS = 32
CAP = 1


def span_parts(key):
    positions = jnp.arange(ST)
    within = positions % BLK
    span_width = jax.random.randint(jax.random.fold_in(key, 21), (ST,), 1, SPAN_MAX + 1)
    span_width = jnp.where(within == 0, SPAN_MAX, span_width)
    jitter = jax.random.randint(jax.random.fold_in(key, 22), (ST,), 0, 3)
    jitter = jnp.where(within == 0, 0, jitter)
    anchor = within * (NB * BLK - SPAN_MAX) // (BLK - 1) + jitter
    first_row = jnp.minimum(anchor, NB * BLK - span_width)
    return (first_row, first_row + span_width)


def draw_span_begin(key, part):
    first_row, last_row = span_parts(key)
    return first_row.astype(jnp.int32)


def draw_span_stop(key, part):
    first_row, last_row = span_parts(key)
    return last_row.astype(jnp.int32)


def draw_block_map(key, part):
    key = jax.random.fold_in(key, 11)
    device_total = ST // S_DEV
    requests = S_DEV // BLK * NB
    local_count = T_DEV // BLK
    key_list = jax.random.split(key, device_total + 1)
    orders = jax.vmap(lambda item: jax.random.permutation(item, device_total))(key_list[:device_total])
    group_slot = jnp.arange(requests) // CAP
    holder = orders[:, group_slot]
    local_pick = jax.random.randint(key_list[device_total], (device_total, requests), 0, local_count)
    return (holder * local_count + local_pick).reshape(SBLOCKS, NB).astype(jnp.int32)


def draw_student(key, part):
    key = jax.random.fold_in(key, 5)
    values = jnp.clip(jax.random.normal(key, (ST, DS), jnp.float32), -5.0, 5.0)
    return values.astype(jnp.bfloat16)


def steps_of(stream_key, shape, pieces, least, top_value):
    def one(dim, blocks):
        heights = jax.random.uniform(jax.random.fold_in(jax.random.fold_in(stream_key, 6), dim), (blocks,), jnp.float32, least / len(pieces), top_value / len(pieces))
        return jnp.repeat(jnp.exp(heights), shape[dim] // blocks).reshape((-1,) + (1,) * (len(shape) - dim - 1))

    level = one(*pieces[0])
    for cut in pieces[1:]:
        level = level * one(*cut)
    return level


def normal_values(stream_key, extent, spread, limit, shards=(), held_as=jnp.bfloat16):
    result = jax.random.normal(stream_key, extent, jnp.float32) * spread
    if len(shards) > 0:
        result = steps_of(stream_key, extent, shards, -0.22, 0.18) * result
    return jnp.clip(result, min=-limit, max=limit).astype(held_as)


def setup_inputs(seed: int = 0, part: int = 0) -> dict:
    splits = jax.random.split(jax.random.key(seed), 8)
    part_keys = jax.random.split(jax.random.fold_in(splits[7], part), 8)
    student = draw_student(jax.random.fold_in(jax.random.fold_in(splits[7], part), 71), part)
    teacher = normal_values(part_keys[1], (TT, DT), 1.0, 6.0, ((0, 16),))
    weight = normal_values(splits[2], (DT, DS), DT ** -0.5, 0.09375, ((0, 16),))
    cotangent = normal_values(part_keys[3], (ST, DS), 1.0, 6.0, ((0, 16),))
    block_map = draw_block_map(jax.random.fold_in(jax.random.fold_in(splits[7], part), 71), part)
    span_begin = draw_span_begin(jax.random.fold_in(jax.random.fold_in(splits[7], part), 71), part)
    span_stop = draw_span_stop(jax.random.fold_in(jax.random.fold_in(splits[7], part), 71), part)
    return {"student": student, "teacher": teacher, "weight": weight, "cotangent": cotangent, "block_map": block_map, "span_begin": span_begin, "span_stop": span_stop}


SCORE_FLOOR = -1.0e30


def attention_pass(queries, key_rows, grad_out, span_first, span_last, score_scale):
    position = jnp.arange(key_rows.shape[1])
    inside = (position[None, None, :] >= span_first[:, :, None]) & (position[None, None, :] < span_last[:, :, None])
    inside = inside[:, None, :, :]
    query_wide = queries.astype(jnp.float32)
    keys_wide = key_rows.astype(jnp.float32)
    grad_wide = grad_out.astype(jnp.float32)
    scores = jnp.einsum("bihd,bjhd->bhij", query_wide, keys_wide) * score_scale
    scores = jnp.where(inside, scores, SCORE_FLOOR)
    row_max = jnp.max(scores, axis=3, keepdims=True)
    raised = jnp.where(inside, jnp.exp(scores - row_max), 0.0)
    attention = raised / jnp.sum(raised, axis=3, keepdims=True)
    attention_low = lax.optimization_barrier(attention.astype(jnp.bfloat16)).astype(jnp.float32)
    output = jnp.einsum("bhij,bjhd->bihd", attention_low, keys_wide).astype(jnp.bfloat16)
    pulled = jnp.einsum("bihd,bjhd->bhij", grad_wide, keys_wide)
    centre = jnp.sum(attention * pulled, axis=3, keepdims=True)
    score_grad = lax.optimization_barrier((attention * (pulled - centre) * score_scale).astype(jnp.bfloat16)).astype(jnp.float32)
    grad_query = jnp.einsum("bhij,bjhd->bihd", score_grad, keys_wide).astype(jnp.bfloat16)
    grad_keys = (jnp.einsum("bhij,bihd->bjhd", score_grad, query_wide) + jnp.einsum("bhij,bihd->bjhd", attention_low, grad_wide)).astype(jnp.bfloat16)
    return output, grad_query, grad_keys


def reference(student, teacher, weight, cotangent, block_map, span_begin, span_stop):
    projected = jnp.dot(teacher, weight, preferred_element_type=jnp.float32).astype(jnp.bfloat16)
    head_count = DS // HEAD
    score_scale = HEAD ** -0.5
    teacher_blocks = projected.reshape(TBLOCKS, BLK, DS)

    def one_block(items):
        queries, grads_out, picks, first_rows, last_rows = items
        key_rows = jnp.take(teacher_blocks, picks.astype(jnp.int32), axis=0).reshape(1, NB * BLK, head_count, HEAD)
        output, query_grad, key_grad = attention_pass(
            queries.reshape(1, BLK, head_count, HEAD), key_rows,
            grads_out.reshape(1, BLK, head_count, HEAD),
            first_rows.reshape(1, BLK), last_rows.reshape(1, BLK), score_scale)
        return output.reshape(BLK, DS), query_grad.reshape(BLK, DS), key_grad.reshape(NB, BLK, DS)

    attended, student_grad, key_grads = lax.map(one_block, (
        student.reshape(SBLOCKS, BLK, DS), cotangent.reshape(SBLOCKS, BLK, DS), block_map,
        span_begin.reshape(SBLOCKS, BLK), span_stop.reshape(SBLOCKS, BLK)))
    projected_grad = jnp.zeros((TBLOCKS, BLK, DS), jnp.float32).at[block_map.reshape(-1).astype(jnp.int32)].add(
        key_grads.reshape(SBLOCKS * NB, BLK, DS).astype(jnp.float32))
    weight_grad = jnp.dot(teacher.astype(jnp.float32).T, projected_grad.reshape(TT, DS),
                          precision=lax.Precision.HIGHEST, preferred_element_type=jnp.float32)
    return attended.reshape(ST, DS), student_grad.reshape(ST, DS), weight_grad
```

```python
import functools

import jax
import jax.numpy as jnp
from jax import lax
from jax.experimental import pallas as pl
from jax.experimental.pallas import tpu as pltpu
from jax.sharding import PartitionSpec as P

HEAD = 128
BLK = 128
NB = 2
SUBS = 2
MESH = pl.DeviceIdType.MESH
SCORE_FLOOR = -1e30
VMEM_BYTES = 56 * 1024 * 1024


def ring_place(chips, snake, chip):
    if not snake:
        return chip
    z, x = chip // 2, chip % 2
    return z * (1 - x) + (chips - 1 - z) * x


def chip_at(chips, snake, place):
    if not snake:
        return place
    down = place // (chips // 2)
    return (1 - down) * (2 * place) + down * (2 * (chips - 1 - place) + 1)


def neighbours(chips, snake):
    me = lax.axis_index("seq")
    core = me % 2
    place = ring_place(chips, snake, me // 2)
    right = chip_at(chips, snake, (place + 1) % chips) * 2 + core
    left = chip_at(chips, snake, (place + chips - 1) % chips) * 2 + core
    sibling = me + 1 - 2 * core
    return me, core, place, (right, left), sibling


def enter(devices):
    barrier = pltpu.get_barrier_semaphore()
    for device in devices:
        pl.semaphore_signal(barrier, inc=1, device_id={"seq": device}, device_id_type=MESH)
    pl.semaphore_wait(barrier, len(devices))


def send(src, dst, send_sem, recv_sem, device):
    copy = pltpu.make_async_remote_copy(
        src_ref=src, dst_ref=dst, send_sem=send_sem, recv_sem=recv_sem,
        device_id={"seq": device}, device_id_type=MESH,
    )
    copy.start()
    return copy


def gather_kernel(chips, snake, x_ref, o_ref, own_sem, ring_send, ring_recv, pair_send, pair_recv):
    me, core, place, beside, sibling = neighbours(chips, snake)
    half = x_ref.shape[0] // 2
    part = half // SUBS
    enter((*beside, sibling))
    own = pltpu.make_async_copy(x_ref, o_ref.at[me], own_sem)
    own.start()
    ring, pair = {}, []
    for s in range(chips):
        for u in range(SUBS):
            for d in range(2):
                from_place = (place + chips - s) % chips if d == 0 else (place + s) % chips
                owner = chip_at(chips, snake, from_place) * 2 + core
                window = pl.ds(d * half + u * part, part)
                dst = o_ref.at[owner, window]
                src = x_ref.at[window] if s == 0 else dst
                if s > 0:
                    ring[d, s - 1, u].wait_recv()
                if s < chips - 1:
                    ring[d, s, u] = send(
                        src, dst, ring_send.at[d, s, u], ring_recv.at[d, s, u], beside[d]
                    )
                pair.append(
                    send(src, dst, pair_send.at[d, s, u], pair_recv.at[d, s, u], sibling)
                )
    own.wait()
    for copy in ring.values():
        copy.wait_send()
    for copy in pair:
        copy.wait()


def gather(x, chips, snake, collective_id):
    sems = [pltpu.SemaphoreType.DMA((2, chips, SUBS)) for _ in range(4)]
    return pl.pallas_call(
        functools.partial(gather_kernel, chips, snake),
        out_shape=jax.ShapeDtypeStruct((2 * chips, *x.shape), x.dtype),
        in_specs=[pl.BlockSpec(memory_space=pl.ANY)],
        out_specs=pl.BlockSpec(memory_space=pl.ANY),
        scratch_shapes=[pltpu.SemaphoreType.DMA, *sems],
        compiler_params=pltpu.CompilerParams(collective_id=collective_id, has_side_effects=True),
    )(x)


def reduce_kernel(
    chips, snake, x_ref, t_ref, o_ref, own, other, landed, landed_w, lhs, grads, term,
    own_sem, pair_send, pair_recv, ring_send, ring_recv, wide_send, wide_recv,
    t_sem, t_send, t_recv, g_send, g_recv,
):
    me, core, place, beside, sibling = neighbours(chips, snake)
    rows, width = x_ref.shape[1:]
    half = rows // 2
    part = half // SUBS
    enter((*beside, sibling))
    t_own = pltpu.make_async_copy(t_ref.at[core], lhs.at[core], t_sem)
    t_own.start()

    def target(d, s):
        if d == 0:
            return chip_at(chips, snake, (place + 2 * chips - 1 - s) % chips)
        return chip_at(chips, snake, (place + 1 + s) % chips)

    local, pair = {}, {}
    for s in range(chips):
        for d in range(2):
            window = pl.ds(d * half, half)
            local[d, s] = pltpu.make_async_copy(
                x_ref.at[target(d, s) * 2 + core, window], own.at[d, s], own_sem.at[d, s]
            )
            local[d, s].start()
            pair[d, s] = send(
                x_ref.at[target(d, s) * 2 + 1 - core, window], other.at[d, s],
                pair_send.at[d, s], pair_recv.at[d, s], sibling,
            )
    t_pair = send(t_ref.at[1 - core], lhs.at[core], t_send, t_recv, sibling)

    ring = {}
    for s in range(chips):
        for d in range(2):
            local[d, s].wait()
            pair[d, s].wait_recv()
        for u in range(SUBS):
            for d in range(2):
                if s > 0:
                    ring[d, s - 1, u].wait_recv()

                @pl.loop(0, part // 16)
                def _(i):
                    window = pl.ds(pl.multiple_of(u * part + i * 16, 16), 16)
                    total = own[d, s, window, :].astype(jnp.float32)
                    total = total + other[d, s, window, :].astype(jnp.float32)
                    if s > 0:
                        total = total + landed[d, s - 1, window, :].astype(jnp.float32)
                    if s < chips - 1:
                        own[d, s, window, :] = total.astype(jnp.bfloat16)
                    else:
                        place_in = pl.ds(pl.multiple_of(d * half + u * part + i * 16, 16), 16)
                        grads[core, place_in, :] = total.astype(jnp.bfloat16)

                window = pl.ds(u * part, part)
                if s < chips - 1:
                    ring[d, s, u] = send(
                        own.at[d, s, window], landed.at[d, s, window],
                        ring_send.at[d, s, u], ring_recv.at[d, s, u], beside[d],
                    )
    g_pair = send(grads.at[core], grads.at[core], g_send, g_recv, sibling)
    t_own.wait()
    t_pair.wait()
    g_pair.wait()
    for copy in ring.values():
        copy.wait_send()
    for copy in pair.values():
        copy.wait_send()

    deep = o_ref.shape[0]
    half = deep // 2
    part = half // SUBS
    tile = min(512, width)

    def make_term(d, s):
        chip = target(d, s)

        @pl.loop(0, width // tile)
        def _(j):
            columns = pl.ds(pl.multiple_of(j * tile, tile), tile)
            term[d, :, columns] = jnp.dot(
                lhs[0, chip, pl.ds(d * half, half), :], grads[0, :, columns],
                preferred_element_type=jnp.float32,
            ) + jnp.dot(
                lhs[1, chip, pl.ds(d * half, half), :], grads[1, :, columns],
                preferred_element_type=jnp.float32,
            )

    wide = {}
    for s in range(chips):
        for d in range(2):
            make_term(d, s)
        for u in range(SUBS):
            for d in range(2):
                if s > 0:
                    wide[d, s - 1, u].wait_recv()

                @pl.loop(0, part // 16)
                def _(i):
                    window = pl.ds(pl.multiple_of(u * part + i * 16, 16), 16)
                    total = term[d, window, :]
                    if s > 0:
                        total = total + landed_w[d, s - 1, window, :].astype(jnp.float32)
                    if s < chips - 1:
                        own[d, s, window, :] = total.astype(jnp.bfloat16)
                    else:
                        place_in = pl.ds(pl.multiple_of(d * half + u * part + i * 16, 16), 16)
                        o_ref[place_in, :] = total

                window = pl.ds(u * part, part)
                if s < chips - 1:
                    wide[d, s, u] = send(
                        own.at[d, s, window], landed_w.at[d, s, window],
                        wide_send.at[d, s, u], wide_recv.at[d, s, u], beside[d],
                    )
    for copy in wide.values():
        copy.wait_send()


def reduce(terms, features, deep, chips, snake, collective_id):
    _, rows, width = terms.shape
    lhs = features.reshape(rows, chips, 2, deep).transpose(2, 1, 3, 0)
    dma = pltpu.SemaphoreType.DMA
    return pl.pallas_call(
        functools.partial(reduce_kernel, chips, snake),
        out_shape=jax.ShapeDtypeStruct((deep, width), jnp.float32),
        in_specs=[pl.BlockSpec(memory_space=pl.ANY)] * 2,
        out_specs=pl.BlockSpec(memory_space=pltpu.VMEM),
        scratch_shapes=[
            pltpu.VMEM((2, chips, rows // 2, width), jnp.bfloat16),
            pltpu.VMEM((2, chips, rows // 2, width), jnp.bfloat16),
            pltpu.VMEM((2, chips - 1, rows // 2, width), jnp.bfloat16),
            pltpu.VMEM((2, chips - 1, deep // 2, width), jnp.bfloat16),
            pltpu.VMEM((2, chips, deep, rows), jnp.bfloat16),
            pltpu.VMEM((2, rows, width), jnp.bfloat16),
            pltpu.VMEM((2, deep // 2, width), jnp.float32),
            dma((2, chips)), dma((2, chips)), dma((2, chips)),
            dma((2, chips, SUBS)), dma((2, chips, SUBS)),
            dma((2, chips, SUBS)), dma((2, chips, SUBS)),
            dma, dma, dma, dma, dma,
        ],
        compiler_params=pltpu.CompilerParams(
            collective_id=collective_id, has_side_effects=True, vmem_limit_bytes=VMEM_BYTES
        ),
    )(terms, lhs)


def attention_kernel(
    picks, q_ref, c_ref, k0_ref, k1_ref, first_ref, last_ref, zeros_ref,
    out_ref, grad_ref, kg_ref, later,
):
    del picks, zeros_ref
    head_count = q_ref.shape[1] // HEAD
    scale = HEAD ** (-0.5)

    @pl.when(pl.program_id(1) == 0)
    def _():
        row = lax.broadcasted_iota(jnp.int32, (NB * BLK, BLK), 0)
        inside = (row >= first_ref[0]) & (row < last_ref[0])
        across = (((1,), (1,)), ((), ()))
        down = (((0,), (0,)), ((), ()))

        @pl.loop(0, head_count, unroll=2)
        def _(h):
            columns = pl.ds(pl.multiple_of(h * HEAD, HEAD), HEAD)
            q, c = q_ref[:, columns], c_ref[:, columns]
            both = jnp.concatenate([q, c], axis=0)
            keys = jnp.concatenate([k0_ref[0, :, columns], k1_ref[0, :, columns]], axis=0)
            products = lax.dot_general(keys, both, across, preferred_element_type=jnp.float32)
            scores = jnp.where(inside, products[:, :BLK] * scale, SCORE_FLOOR)
            raised = jnp.exp(scores - jnp.max(scores, axis=0, keepdims=True))
            probs = raised * (1.0 / jnp.sum(raised, axis=0, keepdims=True))
            pulled = products[:, BLK:]
            centre = jnp.sum(probs * pulled, axis=0, keepdims=True)
            score_grad = (probs * (pulled - centre) * scale).astype(jnp.bfloat16)
            weights = jnp.concatenate([score_grad, probs.astype(jnp.bfloat16)], axis=1)
            rows = lax.dot_general(weights, keys, down, preferred_element_type=jnp.float32)
            grad_ref[:, columns] = rows[:BLK].astype(jnp.bfloat16)
            out_ref[:, columns] = rows[BLK:].astype(jnp.bfloat16)
            key_grad = jnp.dot(weights, both, preferred_element_type=jnp.float32)
            key_grad = key_grad.astype(jnp.bfloat16)
            kg_ref[0, :, columns] = key_grad[:BLK]
            later[:, columns] = key_grad[BLK:]

    @pl.when(pl.program_id(1) == 1)
    def _():
        kg_ref[0] = later[...]


def attention(student, cotangent, blocks, picks, first, last):
    student_rows, width = student.shape
    query_blocks = student_rows // BLK
    rows = pl.BlockSpec((BLK, width), lambda b, n, picks: (b, 0))
    spans = pl.BlockSpec((1, 1, BLK), lambda b, n, picks: (b, 0, 0))
    return pl.pallas_call(
        attention_kernel,
        grid_spec=pltpu.PrefetchScalarGridSpec(
            num_scalar_prefetch=1,
            grid=(query_blocks, NB),
            in_specs=[
                rows,
                rows,
                pl.BlockSpec((1, BLK, width), lambda b, n, picks: (picks[NB * b], 0, 0)),
                pl.BlockSpec((1, BLK, width), lambda b, n, picks: (picks[NB * b + 1], 0, 0)),
                spans,
                spans,
                pl.BlockSpec(memory_space=pl.ANY),
            ],
            out_specs=[
                rows,
                rows,
                pl.BlockSpec((1, BLK, width), lambda b, n, picks: (picks[NB * b + n], 0, 0)),
            ],
            scratch_shapes=[pltpu.VMEM((BLK, width), jnp.bfloat16)],
        ),
        out_shape=[
            jax.ShapeDtypeStruct(student.shape, jnp.bfloat16),
            jax.ShapeDtypeStruct(student.shape, jnp.bfloat16),
            jax.ShapeDtypeStruct(blocks.shape, jnp.bfloat16),
        ],
        input_output_aliases={7: 2},
        compiler_params=pltpu.CompilerParams(
            dimension_semantics=("arbitrary", "arbitrary"), vmem_limit_bytes=VMEM_BYTES
        ),
    )(
        picks, student, cotangent, blocks, blocks,
        first.reshape(query_blocks, 1, BLK), last.reshape(query_blocks, 1, BLK),
        jnp.zeros(blocks.shape, jnp.bfloat16),
    )


def body(snake, student, teacher, weight, cotangent, block_map, span_begin, span_stop):
    seq_count = lax.axis_size("seq")
    chips = seq_count // 2
    device_index = lax.axis_index("seq")
    width = student.shape[1]
    teacher_rows = teacher.shape[0]
    query_blocks = student.shape[0] // BLK
    features = lax.all_gather(teacher, "mp", axis=1, tiled=True)
    deep = weight.shape[0]
    whole_weight = gather(weight, chips, snake, 1).reshape(seq_count * deep, width)
    projected = jnp.dot(features, whole_weight, preferred_element_type=jnp.float32)
    projected = projected.astype(jnp.bfloat16)
    blocks = gather(projected, chips, snake, 2).reshape(-1, BLK, width)
    picks = lax.dynamic_slice_in_dim(block_map, device_index * query_blocks, query_blocks, 0)
    output, grad_query, terms = attention(
        student, cotangent, blocks, picks.reshape(-1), span_begin, span_stop
    )
    weight_grad = reduce(
        terms.reshape(seq_count, teacher_rows, width), features, deep, chips, snake, 3
    )
    return output, grad_query, weight_grad


def solution(mesh):
    in_specs = (
        P(("groups", "seq"), "mp"),
        P(("groups", "seq"), "mp"),
        P("seq", "mp"),
        P(("groups", "seq"), "mp"),
        P("groups", None),
        P(("groups", "seq")),
        P(("groups", "seq")),
    )
    out_specs = (P(("groups", "seq"), "mp"), P(("groups", "seq"), "mp"), P(("groups", "seq"), "mp"))
    snake = mesh.shape["mp"] == 1
    return jax.shard_map(
        functools.partial(body, snake), mesh=mesh, in_specs=in_specs, out_specs=out_specs,
        check_vma=False,
    )
```

```python
import functools

import jax
import jax.numpy as jnp
from jax import lax
from jax.experimental import pallas as pl
from jax.experimental.pallas import tpu as pltpu
from jax.sharding import PartitionSpec as P

HEAD = 128
BLK = 128
NB = 2
SUBS = 2
UNROLL = (16, 4, 16)
MESH = pl.DeviceIdType.MESH
SCORE_FLOOR = -1e30
VMEM_BYTES = 56 * 1024 * 1024


def ring_place(chips, snake, chip):
    if not snake:
        return chip
    z, x = chip // 2, chip % 2
    return z * (1 - x) + (chips - 1 - z) * x


def chip_at(chips, snake, place):
    if not snake:
        return place
    down = place // (chips // 2)
    return (1 - down) * (2 * place) + down * (2 * (chips - 1 - place) + 1)


def neighbours(chips, snake):
    me = lax.axis_index("seq")
    core = me % 2
    place = ring_place(chips, snake, me // 2)
    right = chip_at(chips, snake, (place + 1) % chips) * 2 + core
    left = chip_at(chips, snake, (place + chips - 1) % chips) * 2 + core
    sibling = me + 1 - 2 * core
    return me, core, place, (right, left), sibling


def enter(devices):
    barrier = pltpu.get_barrier_semaphore()
    for device in devices:
        pl.semaphore_signal(barrier, inc=1, device_id={"seq": device}, device_id_type=MESH)
    pl.semaphore_wait(barrier, len(devices))


def send(src, dst, send_sem, recv_sem, device):
    copy = pltpu.make_async_remote_copy(
        src_ref=src, dst_ref=dst, send_sem=send_sem, recv_sem=recv_sem,
        device_id={"seq": device}, device_id_type=MESH,
    )
    copy.start()
    return copy


def gather_kernel(chips, snake, x_ref, o_ref, own_sem, ring_send, ring_recv, pair_send, pair_recv):
    me, core, place, beside, sibling = neighbours(chips, snake)
    half = x_ref.shape[0] // 2
    part = half // SUBS
    enter((*beside, sibling))
    own = pltpu.make_async_copy(x_ref, o_ref.at[me], own_sem)
    own.start()
    ring, pair = {}, []
    for s in range(chips):
        for u in range(SUBS):
            for d in range(2):
                from_place = (place + chips - s) % chips if d == 0 else (place + s) % chips
                owner = chip_at(chips, snake, from_place) * 2 + core
                window = pl.ds(d * half + u * part, part)
                dst = o_ref.at[owner, window]
                src = x_ref.at[window] if s == 0 else dst
                if s > 0:
                    ring[d, s - 1, u].wait_recv()
                if s < chips - 1:
                    ring[d, s, u] = send(
                        src, dst, ring_send.at[d, s, u], ring_recv.at[d, s, u], beside[d]
                    )
                pair.append(
                    send(src, dst, pair_send.at[d, s, u], pair_recv.at[d, s, u], sibling)
                )
    own.wait()
    for copy in ring.values():
        copy.wait_send()
    for copy in pair:
        copy.wait()


def gather(x, chips, snake, collective_id):
    sems = [pltpu.SemaphoreType.DMA((2, chips, SUBS)) for _ in range(4)]
    return pl.pallas_call(
        functools.partial(gather_kernel, chips, snake),
        out_shape=jax.ShapeDtypeStruct((2 * chips, *x.shape), x.dtype),
        in_specs=[pl.BlockSpec(memory_space=pl.ANY)],
        out_specs=pl.BlockSpec(memory_space=pl.ANY),
        scratch_shapes=[pltpu.SemaphoreType.DMA, *sems],
        compiler_params=pltpu.CompilerParams(collective_id=collective_id, has_side_effects=True),
    )(x)


def reduce_kernel(
    chips, snake, x_ref, t_ref, o_ref, own, other, landed, landed_w, lhs, grads, term,
    own_sem, pair_send, pair_recv, ring_send, ring_recv, wide_send, wide_recv,
    t_sem, t_send, t_recv, g_send, g_recv,
):
    me, core, place, beside, sibling = neighbours(chips, snake)
    rows, width = x_ref.shape[1:]
    half = rows // 2
    part = half // SUBS
    enter((*beside, sibling))
    t_own = pltpu.make_async_copy(t_ref.at[core], lhs.at[core], t_sem)
    t_own.start()

    def target(d, s):
        if d == 0:
            return chip_at(chips, snake, (place + 2 * chips - 1 - s) % chips)
        return chip_at(chips, snake, (place + 1 + s) % chips)

    local, pair = {}, {}
    for s in range(chips):
        for d in range(2):
            window = pl.ds(d * half, half)
            local[d, s] = pltpu.make_async_copy(
                x_ref.at[target(d, s) * 2 + core, window], own.at[d, s], own_sem.at[d, s]
            )
            local[d, s].start()
            pair[d, s] = send(
                x_ref.at[target(d, s) * 2 + 1 - core, window], other.at[d, s],
                pair_send.at[d, s], pair_recv.at[d, s], sibling,
            )
    t_pair = send(t_ref.at[1 - core], lhs.at[core], t_send, t_recv, sibling)

    ring = {}
    for s in range(chips):
        for d in range(2):
            local[d, s].wait()
            pair[d, s].wait_recv()
        for u in range(SUBS):
            for d in range(2):
                if s > 0:
                    ring[d, s - 1, u].wait_recv()

                @pl.loop(0, part // 16)
                def _(i):
                    window = pl.ds(pl.multiple_of(u * part + i * 16, 16), 16)
                    total = own[d, s, window, :].astype(jnp.float32)
                    total = total + other[d, s, window, :].astype(jnp.float32)
                    if s > 0:
                        total = total + landed[d, s - 1, window, :].astype(jnp.float32)
                    if s < chips - 1:
                        own[d, s, window, :] = total.astype(jnp.bfloat16)
                    else:
                        place_in = pl.ds(pl.multiple_of(d * half + u * part + i * 16, 16), 16)
                        grads[core, place_in, :] = total.astype(jnp.bfloat16)

                window = pl.ds(u * part, part)
                if s < chips - 1:
                    ring[d, s, u] = send(
                        own.at[d, s, window], landed.at[d, s, window],
                        ring_send.at[d, s, u], ring_recv.at[d, s, u], beside[d],
                    )
    g_pair = send(grads.at[core], grads.at[core], g_send, g_recv, sibling)
    t_own.wait()
    t_pair.wait()
    g_pair.wait()
    for copy in ring.values():
        copy.wait_send()
    for copy in pair.values():
        copy.wait_send()

    deep = o_ref.shape[0]
    half = deep // 2
    part = half // SUBS
    tile = min(512, width)

    def make_term(d, s):
        chip = target(d, s)

        @pl.loop(0, width // tile)
        def _(j):
            columns = pl.ds(pl.multiple_of(j * tile, tile), tile)
            term[d, :, columns] = jnp.dot(
                lhs[0, chip, pl.ds(d * half, half), :], grads[0, :, columns],
                preferred_element_type=jnp.float32,
            ) + jnp.dot(
                lhs[1, chip, pl.ds(d * half, half), :], grads[1, :, columns],
                preferred_element_type=jnp.float32,
            )

    wide = {}
    for s in range(chips):
        for d in range(2):
            make_term(d, s)
        for u in range(SUBS):
            for d in range(2):
                if s > 0:
                    wide[d, s - 1, u].wait_recv()

                @pl.loop(0, part // 16)
                def _(i):
                    window = pl.ds(pl.multiple_of(u * part + i * 16, 16), 16)
                    total = term[d, window, :]
                    if s > 0:
                        total = total + landed_w[d, s - 1, window, :].astype(jnp.float32)
                    if s < chips - 1:
                        own[d, s, window, :] = total.astype(jnp.bfloat16)
                    else:
                        place_in = pl.ds(pl.multiple_of(d * half + u * part + i * 16, 16), 16)
                        o_ref[place_in, :] = total

                window = pl.ds(u * part, part)
                if s < chips - 1:
                    wide[d, s, u] = send(
                        own.at[d, s, window], landed_w.at[d, s, window],
                        wide_send.at[d, s, u], wide_recv.at[d, s, u], beside[d],
                    )
    for copy in wide.values():
        copy.wait_send()


def reduce(terms, features, deep, chips, snake, collective_id):
    _, rows, width = terms.shape
    lhs = features.reshape(rows, chips, 2, deep).transpose(2, 1, 3, 0)
    dma = pltpu.SemaphoreType.DMA
    return pl.pallas_call(
        functools.partial(reduce_kernel, chips, snake),
        out_shape=jax.ShapeDtypeStruct((deep, width), jnp.float32),
        in_specs=[pl.BlockSpec(memory_space=pl.ANY)] * 2,
        out_specs=pl.BlockSpec(memory_space=pltpu.VMEM),
        scratch_shapes=[
            pltpu.VMEM((2, chips, rows // 2, width), jnp.bfloat16),
            pltpu.VMEM((2, chips, rows // 2, width), jnp.bfloat16),
            pltpu.VMEM((2, chips - 1, rows // 2, width), jnp.bfloat16),
            pltpu.VMEM((2, chips - 1, deep // 2, width), jnp.bfloat16),
            pltpu.VMEM((2, chips, deep, rows), jnp.bfloat16),
            pltpu.VMEM((2, rows, width), jnp.bfloat16),
            pltpu.VMEM((2, deep // 2, width), jnp.float32),
            dma((2, chips)), dma((2, chips)), dma((2, chips)),
            dma((2, chips, SUBS)), dma((2, chips, SUBS)),
            dma((2, chips, SUBS)), dma((2, chips, SUBS)),
            dma, dma, dma, dma, dma,
        ],
        compiler_params=pltpu.CompilerParams(
            collective_id=collective_id, has_side_effects=True, vmem_limit_bytes=VMEM_BYTES
        ),
    )(terms, lhs)


def attention_kernel(
    picks, q_ref, c_ref, k0_ref, k1_ref, first_ref, last_ref,
    out_ref, grad_ref, kg_ref, held, empty, products, weights, held_sem, empty_sem,
):
    head_count = q_ref.shape[1] // HEAD
    scale = HEAD ** (-0.5)
    step, steps = pl.program_id(0), pl.num_programs(0)
    slot = step % 2
    share = kg_ref.shape[0] // (picks.shape[0] // NB)

    def leaving(at, n):
        return pltpu.make_async_copy(
            held.at[at % 2, n], kg_ref.at[picks[NB * at + n]], held_sem.at[at % 2, n]
        )

    def filling(m):
        return pltpu.make_async_copy(empty, kg_ref.at[step * share + m], empty_sem.at[m])

    def unread(m):
        named = picks[0] == step * share + m
        for i in range(1, picks.shape[0]):
            named = named | (picks[i] == step * share + m)
        return jnp.logical_not(named)

    @pl.when(step == 0)
    def _():
        empty[...] = jnp.zeros_like(empty)

    for m in range(share):
        @pl.when(unread(m))
        def _():
            filling(m).start()

    @pl.when(step >= 2)
    def _():
        for n in range(NB):
            leaving(step - 2, n).wait()

    row = lax.broadcasted_iota(jnp.int32, (NB * BLK, BLK), 0)
    inside = (row >= first_ref[0]) & (row < last_ref[0])
    across = (((1,), (1,)), ((), ()))
    down = (((0,), (0,)), ((), ()))

    def columns_of(h):
        return pl.ds(pl.multiple_of(h * HEAD, HEAD), HEAD)

    def keys_of(h):
        columns = columns_of(h)
        return jnp.concatenate([k0_ref[0, :, columns], k1_ref[0, :, columns]], axis=0)

    def rows_of(h):
        columns = columns_of(h)
        return jnp.concatenate([q_ref[:, columns], c_ref[:, columns]], axis=0)

    @pl.loop(0, head_count, unroll=min(UNROLL[0], head_count))
    def _(h):
        products[h] = lax.dot_general(
            keys_of(h), rows_of(h), across, preferred_element_type=jnp.float32
        )

    @pl.loop(0, head_count, unroll=min(UNROLL[1], head_count))
    def _(h):
        scores = jnp.where(inside, products[h, :, :BLK] * scale, SCORE_FLOOR)
        raised = jnp.exp(scores - jnp.max(scores, axis=0, keepdims=True))
        probs = raised * (1.0 / jnp.sum(raised, axis=0, keepdims=True))
        pulled = products[h, :, BLK:]
        centre = jnp.sum(probs * pulled, axis=0, keepdims=True)
        weights[h, :, :BLK] = (probs * (pulled - centre) * scale).astype(jnp.bfloat16)
        weights[h, :, BLK:] = probs.astype(jnp.bfloat16)

    @pl.loop(0, head_count, unroll=min(UNROLL[2], head_count))
    def _(h):
        columns = columns_of(h)
        rows = lax.dot_general(weights[h], keys_of(h), down, preferred_element_type=jnp.float32)
        grad_ref[:, columns] = rows[:BLK].astype(jnp.bfloat16)
        out_ref[:, columns] = rows[BLK:].astype(jnp.bfloat16)
        key_grad = jnp.dot(weights[h], rows_of(h), preferred_element_type=jnp.float32)
        key_grad = key_grad.astype(jnp.bfloat16)
        held[slot, 0, :, columns] = key_grad[:BLK]
        held[slot, 1, :, columns] = key_grad[BLK:]

    for n in range(NB):
        leaving(step, n).start()

    for m in range(share):
        @pl.when(unread(m))
        def _():
            filling(m).wait()

    @pl.when(step == steps - 1)
    def _():
        for n in range(NB):
            leaving(step, n).wait()

    @pl.when((step == steps - 1) & (steps > 1))
    def _():
        for n in range(NB):
            leaving(step - 1, n).wait()


def attention(student, cotangent, blocks, picks, first, last):
    student_rows, width = student.shape
    query_blocks = student_rows // BLK
    share = blocks.shape[0] // query_blocks
    rows = pl.BlockSpec((BLK, width), lambda b, picks: (b, 0))
    spans = pl.BlockSpec((1, 1, BLK), lambda b, picks: (b, 0, 0))
    return pl.pallas_call(
        attention_kernel,
        grid_spec=pltpu.PrefetchScalarGridSpec(
            num_scalar_prefetch=1,
            grid=(query_blocks,),
            in_specs=[
                rows,
                rows,
                pl.BlockSpec((1, BLK, width), lambda b, picks: (picks[NB * b], 0, 0)),
                pl.BlockSpec((1, BLK, width), lambda b, picks: (picks[NB * b + 1], 0, 0)),
                spans,
                spans,
            ],
            out_specs=[rows, rows, pl.BlockSpec(memory_space=pl.ANY)],
            scratch_shapes=[
                pltpu.VMEM((2, NB, BLK, width), jnp.bfloat16),
                pltpu.VMEM((BLK, width), jnp.bfloat16),
                pltpu.VMEM((width // HEAD, NB * BLK, 2 * BLK), jnp.float32),
                pltpu.VMEM((width // HEAD, NB * BLK, 2 * BLK), jnp.bfloat16),
                pltpu.SemaphoreType.DMA((2, NB)),
                pltpu.SemaphoreType.DMA((share,)),
            ],
        ),
        out_shape=[
            jax.ShapeDtypeStruct(student.shape, jnp.bfloat16),
            jax.ShapeDtypeStruct(student.shape, jnp.bfloat16),
            jax.ShapeDtypeStruct(blocks.shape, jnp.bfloat16),
        ],
        compiler_params=pltpu.CompilerParams(
            dimension_semantics=("arbitrary",), vmem_limit_bytes=VMEM_BYTES
        ),
    )(
        picks, student, cotangent, blocks, blocks,
        first.reshape(query_blocks, 1, BLK), last.reshape(query_blocks, 1, BLK),
    )


def body(snake, student, teacher, weight, cotangent, block_map, span_begin, span_stop):
    seq_count = lax.axis_size("seq")
    chips = seq_count // 2
    device_index = lax.axis_index("seq")
    width = student.shape[1]
    teacher_rows = teacher.shape[0]
    query_blocks = student.shape[0] // BLK
    features = lax.all_gather(teacher, "mp", axis=1, tiled=True)
    deep = weight.shape[0]
    whole_weight = gather(weight, chips, snake, 1).reshape(seq_count * deep, width)
    projected = jnp.dot(features, whole_weight, preferred_element_type=jnp.float32)
    projected = projected.astype(jnp.bfloat16)
    blocks = gather(projected, chips, snake, 2).reshape(-1, BLK, width)
    picks = lax.dynamic_slice_in_dim(block_map, device_index * query_blocks, query_blocks, 0)
    output, grad_query, terms = attention(
        student, cotangent, blocks, picks.reshape(-1), span_begin, span_stop
    )
    weight_grad = reduce(
        terms.reshape(seq_count, teacher_rows, width), features, deep, chips, snake, 3
    )
    return output, grad_query, weight_grad


def solution(mesh):
    in_specs = (
        P(("groups", "seq"), "mp"),
        P(("groups", "seq"), "mp"),
        P("seq", "mp"),
        P(("groups", "seq"), "mp"),
        P("groups", None),
        P(("groups", "seq")),
        P(("groups", "seq")),
    )
    out_specs = (P(("groups", "seq"), "mp"), P(("groups", "seq"), "mp"), P(("groups", "seq"), "mp"))
    snake = mesh.shape["mp"] == 1
    return jax.shard_map(
        functools.partial(body, snake), mesh=mesh, in_specs=in_specs, out_specs=out_specs,
        check_vma=False,
    )
```

```python
import functools

import jax
import jax.numpy as jnp
from jax import lax
from jax.experimental import pallas as pl
from jax.experimental.pallas import tpu as pltpu
from jax.sharding import PartitionSpec as P

HEAD = 128
BLK = 128
NB = 2
SUBS = 2
UNROLL = (16, 4, 16)
MESH = pl.DeviceIdType.MESH
SCORE_FLOOR = -1e30
VMEM_BYTES = 56 * 1024 * 1024


def ring_place(chips, snake, chip):
    if not snake:
        return chip
    z, x = chip // 2, chip % 2
    return z * (1 - x) + (chips - 1 - z) * x


def chip_at(chips, snake, place):
    if not snake:
        return place
    down = place // (chips // 2)
    return (1 - down) * (2 * place) + down * (2 * (chips - 1 - place) + 1)


def neighbours(chips, snake):
    me = lax.axis_index("seq")
    core = me % 2
    place = ring_place(chips, snake, me // 2)
    right = chip_at(chips, snake, (place + 1) % chips) * 2 + core
    left = chip_at(chips, snake, (place + chips - 1) % chips) * 2 + core
    sibling = me + 1 - 2 * core
    return me, core, place, ({"seq": right}, {"seq": left}), {"seq": sibling}


def enter(devices):
    barrier = pltpu.get_barrier_semaphore()
    for device in devices:
        pl.semaphore_signal(barrier, inc=1, device_id=device, device_id_type=MESH)
    pl.semaphore_wait(barrier, len(devices))


def send(src, dst, send_sem, recv_sem, device):
    copy = pltpu.make_async_remote_copy(
        src_ref=src, dst_ref=dst, send_sem=send_sem, recv_sem=recv_sem,
        device_id=device, device_id_type=MESH,
    )
    copy.start()
    return copy


def gather_kernel(chips, snake, x_ref, o_ref, own_sem, ring_send, ring_recv, pair_send, pair_recv):
    me, core, place, beside, sibling = neighbours(chips, snake)
    half = x_ref.shape[0] // 2
    part = half // SUBS
    enter((*beside, sibling))
    own = pltpu.make_async_copy(x_ref, o_ref.at[me], own_sem)
    own.start()
    ring, pair = {}, []
    for s in range(chips):
        for u in range(SUBS):
            for d in range(2):
                from_place = (place + chips - s) % chips if d == 0 else (place + s) % chips
                owner = chip_at(chips, snake, from_place) * 2 + core
                window = pl.ds(d * half + u * part, part)
                dst = o_ref.at[owner, window]
                src = x_ref.at[window] if s == 0 else dst
                if s > 0:
                    ring[d, s - 1, u].wait_recv()
                if s < chips - 1:
                    ring[d, s, u] = send(
                        src, dst, ring_send.at[d, s, u], ring_recv.at[d, s, u], beside[d]
                    )
                pair.append(
                    send(src, dst, pair_send.at[d, s, u], pair_recv.at[d, s, u], sibling)
                )
    own.wait()
    for copy in ring.values():
        copy.wait_send()
    for copy in pair:
        copy.wait()


def gather_common_kernel(
    chips, snake, kept, x_ref, o_ref, own_sem, ring_send, ring_recv, pair_send, pair_recv,
    hand_send, hand_recv,
):
    me, core, place, beside, sibling = neighbours(chips, snake)
    group = lax.axis_index("groups")
    across = {"groups": 1 - group}
    half = x_ref.shape[0] // 2
    given = (x_ref.shape[1] - kept) // 2
    columns = (
        pl.ds(0, kept),
        pl.ds(pl.multiple_of(kept + group * given, 128), given),
        pl.ds(pl.multiple_of(kept + (1 - group) * given, 128), given),
    )
    enter((*beside, sibling, across))
    own = pltpu.make_async_copy(x_ref, o_ref.at[me], own_sem)
    own.start()
    ring, pair, hand = {}, [], {}

    def ends(d, s, u):
        from_place = (place + chips - s) % chips if d == 0 else (place + s) % chips
        owner = chip_at(chips, snake, from_place) * 2 + core
        rows = pl.ds(d * half, half)
        dst = o_ref.at[owner, rows, columns[u]]
        return (x_ref.at[rows, columns[u]] if s == 0 else dst), dst

    def to_sibling(d, s, u):
        src, dst = ends(d, s, u)
        pair.append(send(src, dst, pair_send.at[d, s, u], pair_recv.at[d, s, u], sibling))

    def handed(s):
        for d in range(2):
            if s > 0:
                hand[d, s].wait_recv()
            to_sibling(d, s, 2)

    for s in range(chips):
        for u in (1, 0):
            for d in range(2):
                src, dst = ends(d, s, u)
                if s > 0:
                    ring[d, s - 1, u].wait_recv()
                if s < chips - 1:
                    ring[d, s, u] = send(
                        src, dst, ring_send.at[d, s, u], ring_recv.at[d, s, u], beside[d]
                    )
                if u == 1 and s > 0:
                    hand[d, s] = send(src, dst, hand_send.at[d, s], hand_recv.at[d, s], across)
                to_sibling(d, s, u)
        if s > 0:
            handed(s - 1)
    handed(chips - 1)
    own.wait()
    for copy in ring.values():
        copy.wait_send()
    for copy in hand.values():
        copy.wait_send()
    for copy in pair:
        copy.wait()


def gather_common(x, chips, snake, kept, collective_id):
    dma = pltpu.SemaphoreType.DMA
    return pl.pallas_call(
        functools.partial(gather_common_kernel, chips, snake, kept),
        out_shape=jax.ShapeDtypeStruct((2 * chips, *x.shape), x.dtype),
        in_specs=[pl.BlockSpec(memory_space=pl.ANY)],
        out_specs=pl.BlockSpec(memory_space=pl.ANY),
        scratch_shapes=[
            dma, dma((2, chips, 2)), dma((2, chips, 2)), dma((2, chips, 3)), dma((2, chips, 3)),
            dma((2, chips)), dma((2, chips)),
        ],
        compiler_params=pltpu.CompilerParams(collective_id=collective_id, has_side_effects=True),
    )(x)


def gather(x, chips, snake, collective_id):
    sems = [pltpu.SemaphoreType.DMA((2, chips, SUBS)) for _ in range(4)]
    return pl.pallas_call(
        functools.partial(gather_kernel, chips, snake),
        out_shape=jax.ShapeDtypeStruct((2 * chips, *x.shape), x.dtype),
        in_specs=[pl.BlockSpec(memory_space=pl.ANY)],
        out_specs=pl.BlockSpec(memory_space=pl.ANY),
        scratch_shapes=[pltpu.SemaphoreType.DMA, *sems],
        compiler_params=pltpu.CompilerParams(collective_id=collective_id, has_side_effects=True),
    )(x)


def reduce_kernel(
    chips, snake, x_ref, t_ref, o_ref, own, other, landed, landed_w, lhs, grads, term,
    own_sem, pair_send, pair_recv, ring_send, ring_recv, wide_send, wide_recv,
    t_sem, t_send, t_recv, g_send, g_recv,
):
    me, core, place, beside, sibling = neighbours(chips, snake)
    rows, width = x_ref.shape[1:]
    half = rows // 2
    part = half // SUBS
    enter((*beside, sibling))
    t_own = pltpu.make_async_copy(t_ref.at[core], lhs.at[core], t_sem)
    t_own.start()

    def target(d, s):
        if d == 0:
            return chip_at(chips, snake, (place + 2 * chips - 1 - s) % chips)
        return chip_at(chips, snake, (place + 1 + s) % chips)

    local, pair = {}, {}
    for s in range(chips):
        for d in range(2):
            window = pl.ds(d * half, half)
            local[d, s] = pltpu.make_async_copy(
                x_ref.at[target(d, s) * 2 + core, window], own.at[d, s], own_sem.at[d, s]
            )
            local[d, s].start()
            pair[d, s] = send(
                x_ref.at[target(d, s) * 2 + 1 - core, window], other.at[d, s],
                pair_send.at[d, s], pair_recv.at[d, s], sibling,
            )
    t_pair = send(t_ref.at[1 - core], lhs.at[core], t_send, t_recv, sibling)

    ring = {}
    for s in range(chips):
        for d in range(2):
            local[d, s].wait()
            pair[d, s].wait_recv()
        for u in range(SUBS):
            for d in range(2):
                if s > 0:
                    ring[d, s - 1, u].wait_recv()

                @pl.loop(0, part // 16)
                def _(i):
                    window = pl.ds(pl.multiple_of(u * part + i * 16, 16), 16)
                    total = own[d, s, window, :].astype(jnp.float32)
                    total = total + other[d, s, window, :].astype(jnp.float32)
                    if s > 0:
                        total = total + landed[d, s - 1, window, :].astype(jnp.float32)
                    if s < chips - 1:
                        own[d, s, window, :] = total.astype(jnp.bfloat16)
                    else:
                        place_in = pl.ds(pl.multiple_of(d * half + u * part + i * 16, 16), 16)
                        grads[core, place_in, :] = total.astype(jnp.bfloat16)

                window = pl.ds(u * part, part)
                if s < chips - 1:
                    ring[d, s, u] = send(
                        own.at[d, s, window], landed.at[d, s, window],
                        ring_send.at[d, s, u], ring_recv.at[d, s, u], beside[d],
                    )
    g_pair = send(grads.at[core], grads.at[core], g_send, g_recv, sibling)
    t_own.wait()
    t_pair.wait()
    g_pair.wait()
    for copy in ring.values():
        copy.wait_send()
    for copy in pair.values():
        copy.wait_send()

    deep = o_ref.shape[0]
    half = deep // 2
    part = half // SUBS
    tile = min(512, width)

    def make_term(d, s):
        chip = target(d, s)

        @pl.loop(0, width // tile)
        def _(j):
            columns = pl.ds(pl.multiple_of(j * tile, tile), tile)
            term[d, :, columns] = jnp.dot(
                lhs[0, chip, pl.ds(d * half, half), :], grads[0, :, columns],
                preferred_element_type=jnp.float32,
            ) + jnp.dot(
                lhs[1, chip, pl.ds(d * half, half), :], grads[1, :, columns],
                preferred_element_type=jnp.float32,
            )

    wide = {}
    for s in range(chips):
        for d in range(2):
            make_term(d, s)
        for u in range(SUBS):
            for d in range(2):
                if s > 0:
                    wide[d, s - 1, u].wait_recv()

                @pl.loop(0, part // 16)
                def _(i):
                    window = pl.ds(pl.multiple_of(u * part + i * 16, 16), 16)
                    total = term[d, window, :]
                    if s > 0:
                        total = total + landed_w[d, s - 1, window, :].astype(jnp.float32)
                    if s < chips - 1:
                        own[d, s, window, :] = total.astype(jnp.bfloat16)
                    else:
                        place_in = pl.ds(pl.multiple_of(d * half + u * part + i * 16, 16), 16)
                        o_ref[place_in, :] = total

                window = pl.ds(u * part, part)
                if s < chips - 1:
                    wide[d, s, u] = send(
                        own.at[d, s, window], landed_w.at[d, s, window],
                        wide_send.at[d, s, u], wide_recv.at[d, s, u], beside[d],
                    )
    for copy in wide.values():
        copy.wait_send()


def reduce(terms, features, deep, chips, snake, collective_id):
    _, rows, width = terms.shape
    lhs = features.reshape(rows, chips, 2, deep).transpose(2, 1, 3, 0)
    dma = pltpu.SemaphoreType.DMA
    return pl.pallas_call(
        functools.partial(reduce_kernel, chips, snake),
        out_shape=jax.ShapeDtypeStruct((deep, width), jnp.float32),
        in_specs=[pl.BlockSpec(memory_space=pl.ANY)] * 2,
        out_specs=pl.BlockSpec(memory_space=pltpu.VMEM),
        scratch_shapes=[
            pltpu.VMEM((2, chips, rows // 2, width), jnp.bfloat16),
            pltpu.VMEM((2, chips, rows // 2, width), jnp.bfloat16),
            pltpu.VMEM((2, chips - 1, rows // 2, width), jnp.bfloat16),
            pltpu.VMEM((2, chips - 1, deep // 2, width), jnp.bfloat16),
            pltpu.VMEM((2, chips, deep, rows), jnp.bfloat16),
            pltpu.VMEM((2, rows, width), jnp.bfloat16),
            pltpu.VMEM((2, deep // 2, width), jnp.float32),
            dma((2, chips)), dma((2, chips)), dma((2, chips)),
            dma((2, chips, SUBS)), dma((2, chips, SUBS)),
            dma((2, chips, SUBS)), dma((2, chips, SUBS)),
            dma, dma, dma, dma, dma,
        ],
        compiler_params=pltpu.CompilerParams(
            collective_id=collective_id, has_side_effects=True, vmem_limit_bytes=VMEM_BYTES
        ),
    )(terms, lhs)


def attention_kernel(
    picks, q_ref, c_ref, k0_ref, k1_ref, first_ref, last_ref,
    out_ref, grad_ref, kg_ref, held, empty, products, weights, held_sem, empty_sem,
):
    head_count = q_ref.shape[1] // HEAD
    scale = HEAD ** (-0.5)
    step, steps = pl.program_id(0), pl.num_programs(0)
    slot = step % 2
    share = kg_ref.shape[0] // (picks.shape[0] // NB)

    def leaving(at, n):
        return pltpu.make_async_copy(
            held.at[at % 2, n], kg_ref.at[picks[NB * at + n]], held_sem.at[at % 2, n]
        )

    def filling(m):
        return pltpu.make_async_copy(empty, kg_ref.at[step * share + m], empty_sem.at[m])

    def unread(m):
        named = picks[0] == step * share + m
        for i in range(1, picks.shape[0]):
            named = named | (picks[i] == step * share + m)
        return jnp.logical_not(named)

    @pl.when(step == 0)
    def _():
        empty[...] = jnp.zeros_like(empty)

    for m in range(share):
        @pl.when(unread(m))
        def _():
            filling(m).start()

    @pl.when(step >= 2)
    def _():
        for n in range(NB):
            leaving(step - 2, n).wait()

    row = lax.broadcasted_iota(jnp.int32, (NB * BLK, BLK), 0)
    inside = (row >= first_ref[0]) & (row < last_ref[0])
    across = (((1,), (1,)), ((), ()))
    down = (((0,), (0,)), ((), ()))

    def columns_of(h):
        return pl.ds(pl.multiple_of(h * HEAD, HEAD), HEAD)

    def keys_of(h):
        columns = columns_of(h)
        return jnp.concatenate([k0_ref[0, :, columns], k1_ref[0, :, columns]], axis=0)

    def rows_of(h):
        columns = columns_of(h)
        return jnp.concatenate([q_ref[:, columns], c_ref[:, columns]], axis=0)

    @pl.loop(0, head_count, unroll=min(UNROLL[0], head_count))
    def _(h):
        products[h] = lax.dot_general(
            keys_of(h), rows_of(h), across, preferred_element_type=jnp.float32
        )

    @pl.loop(0, head_count, unroll=min(UNROLL[1], head_count))
    def _(h):
        scores = jnp.where(inside, products[h, :, :BLK] * scale, SCORE_FLOOR)
        raised = jnp.exp(scores - jnp.max(scores, axis=0, keepdims=True))
        probs = raised * (1.0 / jnp.sum(raised, axis=0, keepdims=True))
        pulled = products[h, :, BLK:]
        centre = jnp.sum(probs * pulled, axis=0, keepdims=True)
        weights[h, :, :BLK] = (probs * (pulled - centre) * scale).astype(jnp.bfloat16)
        weights[h, :, BLK:] = probs.astype(jnp.bfloat16)

    @pl.loop(0, head_count, unroll=min(UNROLL[2], head_count))
    def _(h):
        columns = columns_of(h)
        rows = lax.dot_general(weights[h], keys_of(h), down, preferred_element_type=jnp.float32)
        grad_ref[:, columns] = rows[:BLK].astype(jnp.bfloat16)
        out_ref[:, columns] = rows[BLK:].astype(jnp.bfloat16)
        key_grad = jnp.dot(weights[h], rows_of(h), preferred_element_type=jnp.float32)
        key_grad = key_grad.astype(jnp.bfloat16)
        held[slot, 0, :, columns] = key_grad[:BLK]
        held[slot, 1, :, columns] = key_grad[BLK:]

    for n in range(NB):
        leaving(step, n).start()

    for m in range(share):
        @pl.when(unread(m))
        def _():
            filling(m).wait()

    @pl.when(step == steps - 1)
    def _():
        for n in range(NB):
            leaving(step, n).wait()

    @pl.when((step == steps - 1) & (steps > 1))
    def _():
        for n in range(NB):
            leaving(step - 1, n).wait()


def attention(student, cotangent, blocks, picks, first, last):
    student_rows, width = student.shape
    query_blocks = student_rows // BLK
    share = blocks.shape[0] // query_blocks
    rows = pl.BlockSpec((BLK, width), lambda b, picks: (b, 0))
    spans = pl.BlockSpec((1, 1, BLK), lambda b, picks: (b, 0, 0))
    return pl.pallas_call(
        attention_kernel,
        grid_spec=pltpu.PrefetchScalarGridSpec(
            num_scalar_prefetch=1,
            grid=(query_blocks,),
            in_specs=[
                rows,
                rows,
                pl.BlockSpec((1, BLK, width), lambda b, picks: (picks[NB * b], 0, 0)),
                pl.BlockSpec((1, BLK, width), lambda b, picks: (picks[NB * b + 1], 0, 0)),
                spans,
                spans,
            ],
            out_specs=[rows, rows, pl.BlockSpec(memory_space=pl.ANY)],
            scratch_shapes=[
                pltpu.VMEM((2, NB, BLK, width), jnp.bfloat16),
                pltpu.VMEM((BLK, width), jnp.bfloat16),
                pltpu.VMEM((width // HEAD, NB * BLK, 2 * BLK), jnp.float32),
                pltpu.VMEM((width // HEAD, NB * BLK, 2 * BLK), jnp.bfloat16),
                pltpu.SemaphoreType.DMA((2, NB)),
                pltpu.SemaphoreType.DMA((share,)),
            ],
        ),
        out_shape=[
            jax.ShapeDtypeStruct(student.shape, jnp.bfloat16),
            jax.ShapeDtypeStruct(student.shape, jnp.bfloat16),
            jax.ShapeDtypeStruct(blocks.shape, jnp.bfloat16),
        ],
        compiler_params=pltpu.CompilerParams(
            dimension_semantics=("arbitrary",), vmem_limit_bytes=VMEM_BYTES
        ),
    )(
        picks, student, cotangent, blocks, blocks,
        first.reshape(query_blocks, 1, BLK), last.reshape(query_blocks, 1, BLK),
    )


def body(snake, student, teacher, weight, cotangent, block_map, span_begin, span_stop):
    seq_count = lax.axis_size("seq")
    chips = seq_count // 2
    device_index = lax.axis_index("seq")
    width = student.shape[1]
    teacher_rows = teacher.shape[0]
    query_blocks = student.shape[0] // BLK
    features = lax.all_gather(teacher, "mp", axis=1, tiled=True)
    deep = weight.shape[0]
    given = width // 128 * 5 // 16 * 128
    if lax.axis_size("groups") == 2 and given > 0:
        whole_weight = gather_common(weight, chips, snake, width - 2 * given, 1)
    else:
        whole_weight = gather(weight, chips, snake, 1)
    whole_weight = whole_weight.reshape(seq_count * deep, width)
    projected = jnp.dot(features, whole_weight, preferred_element_type=jnp.float32)
    projected = projected.astype(jnp.bfloat16)
    blocks = gather(projected, chips, snake, 2).reshape(-1, BLK, width)
    picks = lax.dynamic_slice_in_dim(block_map, device_index * query_blocks, query_blocks, 0)
    output, grad_query, terms = attention(
        student, cotangent, blocks, picks.reshape(-1), span_begin, span_stop
    )
    weight_grad = reduce(
        terms.reshape(seq_count, teacher_rows, width), features, deep, chips, snake, 3
    )
    return output, grad_query, weight_grad


def solution(mesh):
    in_specs = (
        P(("groups", "seq"), "mp"),
        P(("groups", "seq"), "mp"),
        P("seq", "mp"),
        P(("groups", "seq"), "mp"),
        P("groups", None),
        P(("groups", "seq")),
        P(("groups", "seq")),
    )
    out_specs = (P(("groups", "seq"), "mp"), P(("groups", "seq"), "mp"), P(("groups", "seq"), "mp"))
    snake = mesh.shape["mp"] == 1
    return jax.shard_map(
        functools.partial(body, snake), mesh=mesh, in_specs=in_specs, out_specs=out_specs,
        check_vma=False,
    )
```
